32 devices in a mesh: groups: 2 (over y), dp: 16 (over z, x, core).
Axes of the slice: x: 2, y: 2, z: 4, core: 2. Of those that a mesh axis runs over, the one named last changes fastest.
Arguments:
- activations: bfloat16 [4096, 14336], P(('groups', 'dp')), parts along dimension 0, may hold values from -6 to 6
- gradients: bfloat16 [4096, 8192], P(('groups', 'dp')), parts along dimension 0, may hold values from -6 to 6
- proj_in: bfloat16 [64, 14336], replicated, may hold values from -0.046875 to 0.046875
- proj_out: bfloat16 [64, 8192], replicated, may hold values from -0.0625 to 0.0625
- targets: bfloat16 [128, 4096], P(('groups', 'dp')), parts along dimension 0, may hold values from -6 to 6
- token_samples: int32 [4096], P(('groups', 'dp')), parts along dimension 0, may hold values from 0 to 31, as said below
- sample_rows: int32 [64], P('groups'), parts along dimension 0, may hold values from 0 to 31, each once
Outputs:
- scores: float32 [64, 64], P(('groups', 'dp')), parts along dimension 0
The draws below stay inside these ranges and needn't reach their ends.
There are 2 independent parts, one for each index of `groups`. The reference program is written for one: setup_inputs(seed, part) draws one part's arguments, and reference() takes and returns one part's arrays. A program takes and returns all parts, laid end to end along the dimension named above; an argument that names none is the same for every part. Nothing has to cross between parts.
Inputs may be any that keep to these rules, and one draw needn't show every extreme that they name: `token_samples`: sample ids never fall along the 2048 tokens; each sample holds 48 to 80 consecutive tokens, both lengths occur, and the first two samples hold 64 tokens each.
All inputs are finite; a program needn't handle non-finite values.
Results may differ from the reference program's by a relative error of at most 0.0033.
Values may be sent and summed in bfloat16 or wider, within the bound.
A program may use at most 64 MiB of HBM per device.

```python
import jax
import jax.numpy as jnp
from jax import lax

D_IN = 14336
D_OUT = 8192
RANK = 64
MEAN = 64
SPREAD = 16
SAMPLES = 32
TOKENS = 2048
TARGETS = 64


def draw_token_samples(key, part):
    key = jax.random.fold_in(key, 11)
    offsets = jax.random.randint(key, (SAMPLES,), 0, SPREAD + 1)
    numbers = jnp.arange(SAMPLES)
    offsets = jnp.where(numbers <= 2, 0, offsets)
    offsets = jnp.where(numbers == 3, SPREAD, offsets)
    offsets = jnp.where(numbers == 4, 0, offsets)
    lengths = MEAN + offsets - jnp.roll(offsets, -1)
    boundary = jnp.cumsum(lengths)
    positions = jnp.arange(TOKENS)
    passed = (boundary[None, :] <= positions[:, None]).astype(jnp.int32)
    return jnp.sum(passed, axis=1).astype(jnp.int32)


def shared_rows(key, sample_ids, width):
    own_rows = jax.random.normal(key, (SAMPLES, width), jnp.float32)
    return own_rows[sample_ids]


def draw_activations(key, part):
    sample_ids = draw_token_samples(key, part)
    key = jax.random.fold_in(key, 23)
    common = shared_rows(jax.random.fold_in(key, 1), sample_ids, D_IN)
    noise = jax.random.normal(jax.random.fold_in(key, 2), (TOKENS, D_IN), jnp.float32)
    values = noise + 0.7 * common
    return jnp.clip(values, -6.0, 6.0).astype(jnp.bfloat16)


def draw_gradients(key, part):
    sample_ids = draw_token_samples(key, part)
    key = jax.random.fold_in(key, 29)
    common = shared_rows(jax.random.fold_in(key, 1), sample_ids, D_OUT)
    noise = jax.random.normal(jax.random.fold_in(key, 2), (TOKENS, D_OUT), jnp.float32)
    values = noise + 0.7 * common
    return jnp.clip(values, -6.0, 6.0).astype(jnp.bfloat16)


def block_levels(own_key, shape, shards, smallest, top_value):
    factor_of, own = 1.0, jax.random.fold_in(own_key, 6)
    for axis_at, shards_of in shards:
        draws = jnp.exp(jax.random.uniform(jax.random.fold_in(own, axis_at), (shards_of,), jnp.float32, smallest / len(shards), top_value / len(shards)))
        factor_of = factor_of * jnp.repeat(draws, shape[axis_at] // shards_of).reshape([-1 if axis == axis_at else 1 for axis in range(len(shape))])
    return factor_of


def bell_draw(own_key, extent, scale, limit, shards=(), dtype=jnp.bfloat16):
    factor_of = block_levels(own_key, extent, shards, -0.22, 0.18) if shards else 1.0
    drawn = jax.random.normal(own_key, extent, jnp.float32) * scale * factor_of
    return jnp.minimum(jnp.maximum(drawn, -limit), limit).astype(dtype)


def setup_inputs(seed: int = 0, part: int = 0) -> dict:
    arg_keys = jax.random.split(jax.random.key(seed), 8)
    part_keys = jax.random.split(jax.random.fold_in(arg_keys[7], part), 8)
    return {
        "activations": draw_activations(jax.random.fold_in(jax.random.fold_in(arg_keys[7], part), 71), part),
        "gradients": draw_gradients(jax.random.fold_in(jax.random.fold_in(arg_keys[7], part), 71), part),
        "proj_in": bell_draw(arg_keys[2], (RANK, D_IN), D_IN ** -0.5, 0.046875),
        "proj_out": bell_draw(arg_keys[3], (RANK, D_OUT), D_OUT ** -0.5, 0.0625),
        "targets": bell_draw(part_keys[4], (TARGETS, RANK * RANK), 1.0, 6.0, ((0, 16),)),
        "token_samples": draw_token_samples(jax.random.fold_in(jax.random.fold_in(arg_keys[7], part), 71), part),
        "sample_rows": jax.random.permutation(part_keys[6], SAMPLES).astype(jnp.int32),
    }


def normalized(values):
    scale = lax.rsqrt(lax.optimization_barrier(jnp.mean(values * values, axis=-1, keepdims=True)) + 1e-06)
    return (values * scale).astype(jnp.bfloat16)

def reference(activations, gradients, proj_in, proj_out, targets, token_samples, sample_rows):
    in_factors = jnp.dot(activations, proj_in.T, preferred_element_type=jnp.float32).astype(jnp.bfloat16)
    out_factors = jnp.dot(gradients, proj_out.T, preferred_element_type=jnp.float32).astype(jnp.bfloat16)
    products = out_factors.astype(jnp.float32)[:, :, None] * in_factors.astype(jnp.float32)[:, None, :]
    products = products.reshape(TOKENS, RANK * RANK)
    sketch = jax.ops.segment_sum(products, token_samples, num_segments=SAMPLES)
    unit_sketch = normalized(sketch)
    placed = jnp.zeros((SAMPLES, RANK * RANK), jnp.bfloat16).at[sample_rows].set(unit_sketch)
    return jnp.dot(placed, targets.T, preferred_element_type=jnp.float32) / RANK
```

```python
import functools

import jax
import jax.numpy as jnp
from jax import lax
from jax.experimental import pallas as pl
from jax.experimental.pallas import tpu as pltpu
from jax.sharding import PartitionSpec as P

MESH = pl.DeviceIdType.MESH
SLOTS = 4
HEAD = 80
QUARTERS = 4
CHUNK = 2048
NT = (((1,), (1,)), ((), ()))
NN = (((1,), (0,)), ((), ()))


def iota(shape, dim):
    return lax.broadcasted_iota(jnp.int32, shape, dim)


def kernel(
    n, act_ref, grad_ref, pin_ref, pout_ref, tgt_ref, tok_ref, rows_ref, out_ref,
    act, grad, pin, pout, stage, table, ids, ids_next, ids_prev, comb, comb_next, sent, arrived,
    load_sem, gather_send, gather_recv, near_send, near_recv, last_send, last_recv,
):
    me = lax.axis_index("dp")
    tokens = act_ref.shape[0]
    rank = pin_ref.shape[0]
    outer, inner = 4, n // 8
    mid_step, outer_step = 2, n // 4
    core = lax.rem(me, 2)
    mid = lax.rem(me // 2, inner)
    out_at = me // outer_step

    barrier = pltpu.get_barrier_semaphore()

    def greet(k, carry):
        pl.semaphore_signal(
            barrier, inc=1, device_id={"dp": lax.rem(me + k, n)}, device_id_type=MESH
        )
        return carry

    lax.fori_loop(1, n, greet, 0)

    loads = []
    for source, proj, source_v, proj_v in (
        (grad_ref, pout_ref, grad, pout),
        (act_ref, pin_ref, act, pin),
    ):
        group = []
        for start in range(0, source.shape[1], CHUNK):
            at = pl.ds(start, CHUNK)
            for src, dst in ((proj, proj_v), (source, source_v)):
                copy = pltpu.make_async_copy(
                    src.at[:, at], dst.at[:, at], load_sem.at[len(loads)]
                )
                copy.start()
                loads.append(copy)
                group.append((copy, start))
    out_chunks = grad_ref.shape[1] // CHUNK

    width = stage.shape[1]
    per = tgt_ref.shape[0]
    for q in range(QUARTERS):
        stage[q * per:(q + 1) * per, :] = tgt_ref[:, q * width:(q + 1) * width].astype(jnp.float32)
    height = QUARTERS * per

    def block_of(index):
        return table.at[pl.ds(pl.multiple_of(index * height, height), height), :]

    table[pl.ds(pl.multiple_of(me * height, height), height), :] = stage[...].astype(jnp.bfloat16)
    ids[...] = jnp.broadcast_to(tok_ref[...], ids.shape)

    pl.semaphore_wait(barrier, n - 1)

    sends = []

    def push(index, device):
        copy = pltpu.make_async_remote_copy(
            src_ref=block_of(index), dst_ref=block_of(index),
            send_sem=gather_send.at[len(sends)], recv_sem=gather_recv.at[index],
            device_id={"dp": device}, device_id_type=MESH,
        )
        copy.start()
        sends.append(copy)

    def await_block(index):
        pltpu.make_async_copy(block_of(index), block_of(index), gather_recv.at[index]).wait()

    def place(o, m, c):
        return o * outer_step + m * mid_step + c

    def near(src, dst, slot, device):
        return pltpu.make_async_remote_copy(
            src_ref=src, dst_ref=dst, send_sem=near_send.at[slot], recv_sem=near_recv.at[slot],
            device_id={"dp": device}, device_id_type=MESH,
        )

    before, after = lax.rem(me + n - 1, n), lax.rem(me + 1, n)
    to_before = near(ids, ids_next, 0, before)
    to_after = near(ids, ids_prev, 1, after)
    head_to_before = near(comb.at[:HEAD, :], comb_next, 2, before)

    other = [lax.rem(out_at + k, outer) for k in range(1, outer)]
    other_mid = [lax.rem(mid + k, inner) for k in range(1, inner)]
    sibling = me + 1 - 2 * core
    for o in other:
        push(me, place(o, mid, core))
    for m in other_mid:
        push(me, place(out_at, m, core))
    push(me, sibling)
    pl.when(me > 0)(to_before.start)
    pl.when(me < n - 1)(to_after.start)

    def forward_outer():
        for o in other:
            index = place(o, mid, core)
            await_block(index)
            for m in other_mid:
                push(index, place(out_at, m, core))
            push(index, sibling)

    def forward_mid():
        for o in [out_at] + other:
            for m in other_mid:
                index = place(o, m, core)
                await_block(index)
                push(index, sibling)

    def factors(first, count, source_v, proj_v):
        total = jnp.zeros((tokens, rank), jnp.float32)
        for k in range(count):
            loads[first + 2 * k].wait()
            loads[first + 2 * k + 1].wait()
            at = slice(k * CHUNK, (k + 1) * CHUNK)
            total += lax.dot_general(
                source_v[:, at], proj_v[:, at], NT, preferred_element_type=jnp.float32
            )
        return total

    out_factors = factors(0, out_chunks, grad, pout)
    in_factors = factors(2 * out_chunks, act_ref.shape[1] // CHUNK, act, pin)
    comb_own = jnp.concatenate([out_factors, in_factors], axis=1)
    comb[...] = comb_own.astype(jnp.bfloat16)
    pl.when(me > 0)(head_to_before.start)
    forward_outer()

    swap_own = pltpu.roll(comb_own, rank, 1).astype(jnp.bfloat16)
    pairs = rank // 2
    lanes = 2 * rank
    pick_row = iota((pairs * 8, lanes), 0) // 8
    pick_lane = iota((pairs * 8, lanes), 1)
    pick = [
        (pick_lane == 2 * pick_row + parity).astype(jnp.float32).astype(jnp.bfloat16)
        for parity in range(2)
    ]
    first = ids[:, 0:1]
    last = ids[:, tokens - 1:tokens]
    low_lanes = iota((pairs * 8, lanes), 1) < rank

    def sketch_part(values, swapped, token_ids):
        count = values.shape[0]
        mask = (token_ids[:, :count] == first + iota((8, count), 0)).astype(jnp.float32)
        parts = []
        for parity, matched in ((0, swapped), (1, values)):
            spread = lax.dot_general(pick[parity], values, NT, preferred_element_type=jnp.float32)
            spread = spread.reshape(pairs, 8, count) * mask[None]
            spread = spread.reshape(pairs * 8, count).astype(jnp.bfloat16)
            parts.append(lax.dot_general(spread, matched, NN, preferred_element_type=jnp.float32))
        return jnp.where(low_lanes, parts[0], parts[1])

    sketch = sketch_part(comb[...], swap_own, ids[...])
    forward_mid()

    @pl.when(me < n - 1)
    def _():
        to_before.wait_recv()
        head_to_before.wait_recv()

    @pl.when(me == n - 1)
    def _():
        ids_next[...] = jnp.full(ids_next.shape, -1, jnp.int32)
        comb_next[...] = jnp.zeros_like(comb_next)

    @pl.when(me > 0)
    def _():
        to_after.wait_recv()

    @pl.when(me == 0)
    def _():
        ids_prev[...] = jnp.full(ids_prev.shape, -1, jnp.int32)

    values = comb_next[...]
    swapped = pltpu.roll(values.astype(jnp.float32), rank, 1).astype(jnp.bfloat16)
    sketch += sketch_part(values, swapped, ids_next[...])
    tiles = sketch.reshape(pairs, 8, lanes)
    total = jnp.sum(jnp.sum(tiles * tiles, axis=0), axis=1, keepdims=True)
    scale = lax.rsqrt(total / (rank * rank) + 1e-06)
    tiles = tiles * scale[None]
    span = pairs // QUARTERS
    unit = jnp.concatenate(
        [
            jnp.concatenate([tiles[q * span + p] for p in range(span)], axis=1)
            for q in range(QUARTERS)
        ],
        axis=0,
    ).astype(jnp.bfloat16)

    for o in range(outer):
        for m in range(inner):
            await_block(place(o, m, 1 - core))
    every = n * height
    mixed = lax.dot_general(unit, table[...], NT, preferred_element_type=jnp.float32)
    quarter_of = lax.rem(iota((8, every), 1) // per, QUARTERS)
    total = jnp.zeros((8, every), jnp.float32)
    for q in range(QUARTERS):
        total += jnp.where(quarter_of == q, mixed[q * 8:(q + 1) * 8], 0.0)
    high = total.astype(jnp.bfloat16).astype(jnp.float32)
    halves = jnp.concatenate([high, total - high], axis=0).astype(jnp.bfloat16)
    columns = sent.shape[2]
    lane = iota((every, columns), 0)
    fold = (lane // height * per + lax.rem(lane, per) == iota((every, columns), 1))
    fold = fold.astype(jnp.float32).astype(jnp.bfloat16)
    folded = lax.dot_general(halves, fold, NN, preferred_element_type=jnp.float32)
    scores = (folded[:8] + folded[8:]) / rank

    samples = rows_ref.shape[1]
    own_rows = samples // n
    goals = []
    for s in range(SLOTS):
        here = first[0:1] + s
        found = jnp.where(iota((1, samples), 1) == here, rows_ref[...], 0)
        goal = jnp.sum(found, axis=1, keepdims=True)
        valid = here <= last[0:1]
        if s == 0:
            valid = valid & (ids_prev[0:1, tokens - 1:tokens] != here)
        goals.append(jnp.where(valid, goal, -1))
    sublane = iota((8, columns), 0)
    position = jnp.where(sublane < own_rows, sublane, samples)
    offsets = [jnp.broadcast_to(goal, (8, columns)) - position for goal in goals]
    lines = [jnp.broadcast_to(scores[s:s + 1], (8, columns)) for s in range(SLOTS)]

    def tile_for(device):
        tile = jnp.zeros((8, columns), jnp.float32)
        for s in range(SLOTS):
            tile += jnp.where(offsets[s] == device * own_rows, lines[s], 0.0)
        return tile

    def last_copy(device, source):
        return pltpu.make_async_remote_copy(
            src_ref=sent.at[device], dst_ref=arrived.at[me],
            send_sem=last_send.at[device], recv_sem=last_recv.at[source],
            device_id={"dp": device}, device_id_type=MESH,
        )

    def deliver(k, carry):
        device = lax.rem(me + k, n)
        sent[device] = tile_for(device)
        last_copy(device, me).start()
        return carry

    lax.fori_loop(1, n, deliver, 0, unroll=n <= 16)
    arrived[me] = tile_for(me)

    def receive(k, carry):
        source = lax.rem(me + k, n)
        pltpu.make_async_copy(arrived.at[source], arrived.at[source], last_recv.at[source]).wait()
        return carry

    lax.fori_loop(1, n, receive, 0, unroll=n <= 16)
    result = jnp.sum(arrived[...], axis=0)
    out_ref[...] = result[:own_rows, :out_ref.shape[1]]

    def sent_off(k, carry):
        device = lax.rem(me + k, n)
        last_copy(device, me).wait_send()
        return carry

    lax.fori_loop(1, n, sent_off, 0, unroll=n <= 16)
    for copy in sends:
        copy.wait_send()

    @pl.when(me > 0)
    def _():
        to_before.wait_send()
        head_to_before.wait_send()

    @pl.when(me < n - 1)
    def _():
        to_after.wait_send()


def on_device(activations, gradients, proj_in, proj_out, targets, token_samples, sample_rows):
    n = lax.axis_size("dp")
    tokens, d_in = activations.shape
    d_out = gradients.shape[1]
    rank = proj_in.shape[0]
    per, square = targets.shape
    samples = sample_rows.shape[0]
    height = QUARTERS * per
    width = square // QUARTERS
    columns = max(128, n * per)
    gather_sends = 3 + 4 * (n // 8 - 1) + n // 2
    vmem = pl.BlockSpec(memory_space=pltpu.VMEM)
    hbm = pl.BlockSpec(memory_space=pl.ANY)
    bf16, f32 = jnp.bfloat16, jnp.float32
    return pl.pallas_call(
        functools.partial(kernel, n),
        out_shape=jax.ShapeDtypeStruct((samples // n, n * per), f32),
        in_specs=[hbm, hbm, hbm, hbm, vmem, vmem, vmem],
        out_specs=vmem,
        scratch_shapes=[
            pltpu.VMEM((tokens, d_in), bf16),
            pltpu.VMEM((tokens, d_out), bf16),
            pltpu.VMEM((rank, d_in), bf16),
            pltpu.VMEM((rank, d_out), bf16),
            pltpu.VMEM((height, width), f32),
            pltpu.VMEM((n * height, width), bf16),
            pltpu.VMEM((8, tokens), jnp.int32),
            pltpu.VMEM((8, tokens), jnp.int32),
            pltpu.VMEM((8, tokens), jnp.int32),
            pltpu.VMEM((tokens, 2 * rank), bf16),
            pltpu.VMEM((HEAD, 2 * rank), bf16),
            pltpu.VMEM((n, 8, columns), f32),
            pltpu.VMEM((n, 8, columns), f32),
            pltpu.SemaphoreType.DMA((2 * (d_in + d_out) // CHUNK,)),
            pltpu.SemaphoreType.DMA((gather_sends,)),
            pltpu.SemaphoreType.DMA((n,)),
            pltpu.SemaphoreType.DMA((3,)),
            pltpu.SemaphoreType.DMA((3,)),
            pltpu.SemaphoreType.DMA((n,)),
            pltpu.SemaphoreType.DMA((n,)),
        ],
        compiler_params=pltpu.CompilerParams(
            collective_id=0, has_side_effects=True, vmem_limit_bytes=56 * 1024 * 1024
        ),
    )(
        activations, gradients, proj_in, proj_out, targets,
        token_samples.reshape(1, tokens), sample_rows.reshape(1, samples),
    )


def solution(mesh):
    in_specs = (
        P(("groups", "dp"), None),
        P(("groups", "dp"), None),
        P(),
        P(),
        P(("groups", "dp"), None),
        P(("groups", "dp")),
        P("groups"),
    )
    out_specs = P(("groups", "dp"), None)
    return jax.shard_map(
        on_device, mesh=mesh, in_specs=in_specs, out_specs=out_specs, check_vma=False
    )
```

```python
import functools

import jax
import jax.numpy as jnp
from jax import lax
from jax.experimental import pallas as pl
from jax.experimental.pallas import tpu as pltpu
from jax.sharding import PartitionSpec as P

MESH = pl.DeviceIdType.MESH
SLOTS = 4
HEAD = 80
QUARTERS = 4
CHUNK = 2048
BEGIN_AT, OUTER_AT = 4, 12
NT = (((1,), (1,)), ((), ()))
NN = (((1,), (0,)), ((), ()))


def iota(shape, dim):
    return lax.broadcasted_iota(jnp.int32, shape, dim)


def kernel(
    n, act_ref, grad_ref, pin_ref, pout_ref, tgt_ref, tok_ref, rows_ref, out_ref,
    act, grad, pin, pout, stage, table, units, goals_all, ids, ids_next, ids_prev, comb, comb_next, sent, arrived,
    load_sem, gather_send, gather_recv, near_send, near_recv, mid_send, mid_recv, last_send, last_recv,
):
    me = lax.axis_index("dp")
    tokens = act_ref.shape[0]
    rank = pin_ref.shape[0]
    outer, inner = 4, n // 8
    mid_step, outer_step = 2, n // 4
    core = lax.rem(me, 2)
    mid = lax.rem(me // 2, inner)
    out_at = me // outer_step

    barrier = pltpu.get_barrier_semaphore()

    def greet(k, carry):
        pl.semaphore_signal(
            barrier, inc=1, device_id={"dp": lax.rem(me + k, n)}, device_id_type=MESH
        )
        return carry

    lax.fori_loop(1, n, greet, 0)

    loads = []
    for source, proj, source_v, proj_v in (
        (grad_ref, pout_ref, grad, pout),
        (act_ref, pin_ref, act, pin),
    ):
        group = []
        for start in range(0, source.shape[1], CHUNK):
            at = pl.ds(start, CHUNK)
            for src, dst in ((proj, proj_v), (source, source_v)):
                copy = pltpu.make_async_copy(
                    src.at[:, at], dst.at[:, at], load_sem.at[len(loads)]
                )
                copy.start()
                loads.append(copy)
                group.append((copy, start))
    out_chunks = grad_ref.shape[1] // CHUNK
    STEPS = out_chunks + act_ref.shape[1] // CHUNK

    pairs = rank // 2
    lanes = 2 * rank
    pick_row = iota((pairs * 8, lanes), 0) >> 3
    pick_lane = iota((pairs * 8, lanes), 1)
    pick = [
        (pick_lane == 2 * pick_row + parity).astype(jnp.float32).astype(jnp.bfloat16)
        for parity in range(2)
    ]

    width = stage.shape[1]
    per = tgt_ref.shape[0]
    for q in range(QUARTERS):
        stage[q * per:(q + 1) * per, :] = tgt_ref[:, q * width:(q + 1) * width].astype(jnp.float32)
    height = QUARTERS * per

    def block_of(index):
        return table.at[pl.ds(pl.multiple_of(index * height, height), height), :]

    own_block = 2 * out_at + core
    table[pl.ds(pl.multiple_of(own_block * height, height), height), :] = stage[...].astype(
        jnp.bfloat16
    )
    ids[...] = jnp.broadcast_to(tok_ref[...], ids.shape)

    sends = []

    def push(index, device):
        copy = pltpu.make_async_remote_copy(
            src_ref=block_of(index), dst_ref=block_of(index),
            send_sem=gather_send.at[len(sends)], recv_sem=gather_recv.at[index],
            device_id={"dp": device}, device_id_type=MESH,
        )
        copy.start()
        sends.append(copy)

    def await_block(index):
        pltpu.make_async_copy(block_of(index), block_of(index), gather_recv.at[index]).wait()

    def place(o, m, c):
        return o * outer_step + m * mid_step + c

    def near(src, dst, slot, device):
        return pltpu.make_async_remote_copy(
            src_ref=src, dst_ref=dst, send_sem=near_send.at[slot], recv_sem=near_recv.at[slot],
            device_id={"dp": device}, device_id_type=MESH,
        )

    before, after = lax.rem(me + n - 1, n), lax.rem(me + 1, n)
    to_before = near(ids, ids_next, 0, before)
    to_after = near(ids, ids_prev, 1, after)
    head_to_before = near(comb.at[:HEAD, :], comb_next, 2, before)

    other = [lax.rem(out_at + k, outer) for k in range(1, outer)]
    other_mid = [lax.rem(mid + k, inner) for k in range(1, inner)]
    sibling = me + 1 - 2 * core

    def begin():
        pl.semaphore_wait(barrier, n - 1)
        for o in other:
            push(own_block, place(o, mid, core))
        push(own_block, sibling)
        pl.when(me > 0)(to_before.start)
        pl.when(me < n - 1)(to_after.start)

    def forward_outer():
        for o in other:
            index = 2 * o + core
            await_block(index)
            push(index, sibling)

    steps = {BEGIN_AT: begin, OUTER_AT: forward_outer}

    def factors(first, count, source_v, proj_v):
        total = jnp.zeros((tokens, rank), jnp.float32)
        for k in range(count):
            steps.get(first // 2 + k, lambda: None)()
            loads[first + 2 * k].wait()
            loads[first + 2 * k + 1].wait()
            at = slice(k * CHUNK, (k + 1) * CHUNK)
            total += lax.dot_general(
                source_v[:, at], proj_v[:, at], NT, preferred_element_type=jnp.float32
            )
        return total

    out_factors = factors(0, out_chunks, grad, pout)
    in_factors = factors(2 * out_chunks, act_ref.shape[1] // CHUNK, act, pin)
    comb_own = jnp.concatenate([out_factors, in_factors], axis=1)
    comb[...] = comb_own.astype(jnp.bfloat16)
    steps.get(STEPS, lambda: None)()
    pl.when(me > 0)(head_to_before.start)
    steps.get(STEPS + 1, lambda: None)()

    swap_own = pltpu.roll(comb_own, rank, 1).astype(jnp.bfloat16)
    first = ids[:, 0:1]
    last = ids[:, tokens - 1:tokens]
    low_lanes = iota((pairs * 8, lanes), 1) < rank

    def sketch_part(values, swapped, token_ids):
        count = values.shape[0]
        mask = (token_ids[:, :count] == first + (iota((8, count), 0) & (SLOTS - 1))).astype(jnp.float32)
        parts = []
        for parity, matched in ((0, swapped), (1, values)):
            spread = lax.dot_general(pick[parity], values, NT, preferred_element_type=jnp.float32)
            spread = spread.reshape(pairs, 8, count) * mask[None]
            spread = spread.reshape(pairs * 8, count).astype(jnp.bfloat16)
            parts.append(lax.dot_general(spread, matched, NN, preferred_element_type=jnp.float32))
        return jnp.where(low_lanes, parts[0], parts[1])

    sketch = sketch_part(comb[...], swap_own, ids[...])
    steps.get(STEPS + 2, lambda: None)()

    @pl.when(me < n - 1)
    def _():
        to_before.wait_recv()

    @pl.when(me == n - 1)
    def _():
        ids_next[...] = jnp.full(ids_next.shape, -1, jnp.int32)
        comb_next[...] = jnp.zeros_like(comb_next)

    @pl.when(me > 0)
    def _():
        to_after.wait_recv()

    @pl.when(me == 0)
    def _():
        ids_prev[...] = jnp.full(ids_prev.shape, -1, jnp.int32)

    samples = rows_ref.shape[1]
    own_rows = samples // n
    for s in range(SLOTS):
        here = first[0:1] + s
        found = jnp.where(iota((1, samples), 1) == here, rows_ref[...], 0)
        goal = jnp.sum(found, axis=1, keepdims=True)
        valid = here <= last[0:1]
        if s == 0:
            valid = valid & (ids_prev[0:1, tokens - 1:tokens] != here)
        goals_all[mid, s:s + 1, :] = jnp.broadcast_to(jnp.where(valid, goal, -1), (1, 128))

    def goal_copy(k, m, source):
        return pltpu.make_async_remote_copy(
            src_ref=goals_all.at[mid], dst_ref=goals_all.at[mid],
            send_sem=mid_send.at[0, k], recv_sem=mid_recv.at[0, source],
            device_id={"dp": place(out_at, m, core)}, device_id_type=MESH,
        )

    rows_of = SLOTS * QUARTERS

    def unit_rows(m):
        return units.at[pl.ds(pl.multiple_of(m * rows_of, rows_of), rows_of), :]

    def unit_copy(k, m, source):
        return pltpu.make_async_remote_copy(
            src_ref=unit_rows(mid), dst_ref=unit_rows(mid),
            send_sem=mid_send.at[1, k], recv_sem=mid_recv.at[1, source],
            device_id={"dp": place(out_at, m, core)}, device_id_type=MESH,
        )

    for k, m in enumerate(other_mid):
        goal_copy(k, m, mid).start()

    @pl.when(me < n - 1)
    def _():
        head_to_before.wait_recv()

    values = comb_next[...]
    swapped = pltpu.roll(values.astype(jnp.float32), rank, 1).astype(jnp.bfloat16)
    sketch += sketch_part(values, swapped, ids_next[...])
    tiles = sketch.reshape(pairs, 8, lanes)
    total = jnp.sum(jnp.sum(tiles * tiles, axis=0), axis=1, keepdims=True)
    scale = lax.rsqrt(total / (rank * rank) + 1e-06)
    tiles = tiles * scale[None]
    span = pairs // QUARTERS
    upper = iota((8, lanes), 0) < SLOTS
    unit = jnp.concatenate(
        [
            jnp.concatenate(
                [
                    jnp.where(upper, tiles[q * span + p], tiles[(q + 1) * span + p])
                    for p in range(span)
                ],
                axis=1,
            )
            for q in range(0, QUARTERS, 2)
        ],
        axis=0,
    ).astype(jnp.bfloat16)
    units[pl.ds(pl.multiple_of(mid * rows_of, rows_of), rows_of), :] = unit
    for k, m in enumerate(other_mid):
        unit_copy(k, m, mid).start()

    every = 2 * outer * height
    columns = sent.shape[2]
    lane = iota((every, columns), 0)
    device_of = lax.rem(lane // height, 2) + lane // (2 * height) * outer_step + mid * mid_step
    fold = device_of * per + lax.rem(lane, per) == iota((every, columns), 1)
    fold = fold.astype(jnp.float32).astype(jnp.bfloat16)
    for o in range(outer):
        await_block(2 * o + 1 - core)
    for k, m in enumerate(other_mid):
        goal_copy(k, m, m).wait_recv()
        pltpu.make_async_copy(unit_rows(m), unit_rows(m), mid_recv.at[1, m]).wait()
    mixed = lax.dot_general(units[...], table[...], NT, preferred_element_type=jnp.float32)
    quarter_row = lax.rem(iota((rows_of, every), 0) // SLOTS, QUARTERS)
    quarter_lane = lax.rem(iota((rows_of, every), 1) // per, QUARTERS)
    same = quarter_row == quarter_lane
    summed = []
    for m in range(inner):
        part = jnp.where(same, mixed[m * rows_of:(m + 1) * rows_of], 0.0)
        part = part[:8] + part[8:]
        summed.append(part + pltpu.roll(part, SLOTS, 0))
    first_half = iota((8, every), 0) < SLOTS
    total = jnp.concatenate(
        [jnp.where(first_half, summed[m], summed[m + 1]) for m in range(0, inner, 2)], axis=0
    )
    slots = inner * SLOTS
    high = total.astype(jnp.bfloat16).astype(jnp.float32)
    halves = jnp.concatenate([high, total - high], axis=0).astype(jnp.bfloat16)
    folded = lax.dot_general(halves, fold, NN, preferred_element_type=jnp.float32)
    scores = (folded[:slots] + folded[slots:]) / rank

    sublane = iota((8, columns), 0)
    position = jnp.where(sublane < own_rows, sublane, samples)
    offsets = [
        jnp.broadcast_to(goals_all[m, s:s + 1, 0:1], (8, columns)) - position
        for m in range(inner)
        for s in range(SLOTS)
    ]
    lines = [jnp.broadcast_to(scores[s:s + 1], (8, columns)) for s in range(slots)]

    def tile_for(device):
        tile = jnp.zeros((8, columns), jnp.float32)
        for s in range(slots):
            tile += jnp.where(offsets[s] == device * own_rows, lines[s], 0.0)
        return tile

    def last_copy(device, source):
        return pltpu.make_async_remote_copy(
            src_ref=sent.at[device], dst_ref=arrived.at[me],
            send_sem=last_send.at[device], recv_sem=last_recv.at[source],
            device_id={"dp": device}, device_id_type=MESH,
        )

    def deliver(k, carry):
        device = lax.rem(me + k, n)
        sent[device] = tile_for(device)
        last_copy(device, me).start()
        return carry

    lax.fori_loop(1, n, deliver, 0, unroll=n <= 16)
    arrived[me] = tile_for(me)

    def receive(k, carry):
        source = lax.rem(me + k, n)
        pltpu.make_async_copy(arrived.at[source], arrived.at[source], last_recv.at[source]).wait()
        return carry

    lax.fori_loop(1, n, receive, 0, unroll=n <= 16)
    result = jnp.sum(arrived[...], axis=0)
    out_ref[...] = result[:own_rows, :out_ref.shape[1]]

    def sent_off(k, carry):
        device = lax.rem(me + k, n)
        last_copy(device, me).wait_send()
        return carry

    lax.fori_loop(1, n, sent_off, 0, unroll=n <= 16)
    for copy in sends:
        copy.wait_send()
    for k, m in enumerate(other_mid):
        goal_copy(k, m, mid).wait_send()
        unit_copy(k, m, mid).wait_send()

    @pl.when(me > 0)
    def _():
        to_before.wait_send()
        head_to_before.wait_send()

    @pl.when(me < n - 1)
    def _():
        to_after.wait_send()


def on_device(activations, gradients, proj_in, proj_out, targets, token_samples, sample_rows):
    n = lax.axis_size("dp")
    tokens, d_in = activations.shape
    d_out = gradients.shape[1]
    rank = proj_in.shape[0]
    per, square = targets.shape
    samples = sample_rows.shape[0]
    height = QUARTERS * per
    width = square // QUARTERS
    columns = max(128, n * per)
    inner = n // 8
    blocks = n // inner
    vmem = pl.BlockSpec(memory_space=pltpu.VMEM)
    hbm = pl.BlockSpec(memory_space=pl.ANY)
    bf16, f32 = jnp.bfloat16, jnp.float32
    return pl.pallas_call(
        functools.partial(kernel, n),
        out_shape=jax.ShapeDtypeStruct((samples // n, n * per), f32),
        in_specs=[hbm, hbm, hbm, hbm, vmem, vmem, vmem],
        out_specs=vmem,
        scratch_shapes=[
            pltpu.VMEM((tokens, d_in), bf16),
            pltpu.VMEM((tokens, d_out), bf16),
            pltpu.VMEM((rank, d_in), bf16),
            pltpu.VMEM((rank, d_out), bf16),
            pltpu.VMEM((height, width), f32),
            pltpu.VMEM((blocks * height, width), bf16),
            pltpu.VMEM((inner * SLOTS * QUARTERS, width), bf16),
            pltpu.VMEM((inner, 8, 128), jnp.int32),
            pltpu.VMEM((8, tokens), jnp.int32),
            pltpu.VMEM((8, tokens), jnp.int32),
            pltpu.VMEM((8, tokens), jnp.int32),
            pltpu.VMEM((tokens, 2 * rank), bf16),
            pltpu.VMEM((HEAD, 2 * rank), bf16),
            pltpu.VMEM((n, 8, columns), f32),
            pltpu.VMEM((n, 8, columns), f32),
            pltpu.SemaphoreType.DMA((2 * (d_in + d_out) // CHUNK,)),
            pltpu.SemaphoreType.DMA((blocks - 1,)),
            pltpu.SemaphoreType.DMA((blocks,)),
            pltpu.SemaphoreType.DMA((3,)),
            pltpu.SemaphoreType.DMA((3,)),
            pltpu.SemaphoreType.DMA((2, inner)),
            pltpu.SemaphoreType.DMA((2, inner)),
            pltpu.SemaphoreType.DMA((n,)),
            pltpu.SemaphoreType.DMA((n,)),
        ],
        compiler_params=pltpu.CompilerParams(
            collective_id=0, has_side_effects=True, vmem_limit_bytes=56 * 1024 * 1024
        ),
    )(
        activations, gradients, proj_in, proj_out, targets,
        token_samples.reshape(1, tokens), sample_rows.reshape(1, samples),
    )


def solution(mesh):
    in_specs = (
        P(("groups", "dp"), None),
        P(("groups", "dp"), None),
        P(),
        P(),
        P(("groups", "dp"), None),
        P(("groups", "dp")),
        P("groups"),
    )
    out_specs = P(("groups", "dp"), None)
    return jax.shard_map(
        on_device, mesh=mesh, in_specs=in_specs, out_specs=out_specs, check_vma=False
    )
```
